32 devices in a mesh: replica: 2 (over x), fsdp: 16 (over z, y, core).
Axes of the slice: x: 2, y: 2, z: 4, core: 2. Of those that a mesh axis runs over, the one named last changes fastest.
Arguments:
- tokens: bfloat16 [2, 4096, 1024], P('replica', 'fsdp'), may hold values from -6 to 6
- segments: int32 [2, 4096], P('replica'), may hold values from 0 to 2, as said below
- cotangent: bfloat16 [2, 4096, 1024], P('replica', 'fsdp'), may hold values from -6 to 6
- norm_gain_one: bfloat16 [1024], P('fsdp'), may hold values from 0.5 to 1.5
- in_weight: bfloat16 [1024, 3328], P('fsdp'), may hold values from -0.1875 to 0.1875
- step_weight: bfloat16 [1024, 24], P('fsdp'), may hold values from -0.1875 to 0.1875
- qkv_weight: bfloat16 [1024, 768], P('fsdp'), may hold values from -0.1875 to 0.1875
- ssm_out_weight: bfloat16 [1536, 1024], P('fsdp'), may hold values from -0.01953125 to 0.01953125
- attn_out_weight: bfloat16 [512, 1024], P('fsdp'), may hold values from -6 to 6
- decay_log: float32 [24], replicated, may hold values from -9 to -1
- step_bias: float32 [24], replicated, may hold values from -4 to -1
- skip_gain: float32 [24], replicated, may hold values from 0.5 to 1.5
- norm_gain_two: bfloat16 [1024], P('fsdp'), may hold values from 0.5 to 1.5
- gate_weight: bfloat16 [1024, 2048], P('fsdp'), may hold values from -0.1875 to 0.1875
- up_weight: bfloat16 [1024, 2048], P('fsdp'), may hold values from -0.1875 to 0.1875
- down_weight: bfloat16 [2048, 1024], P('fsdp'), may hold values from -0.125 to 0.125
Outputs:
- output: bfloat16 [2, 4096, 1024], P('replica', 'fsdp')
- tokens_grad: bfloat16 [2, 4096, 1024], P('replica', 'fsdp')
- norm_gain_one_grad: float32 [1024], P('fsdp')
- in_weight_grad: float32 [1024, 3328], P('fsdp')
- step_weight_grad: float32 [1024, 24], P('fsdp')
- qkv_weight_grad: float32 [1024, 768], P('fsdp')
- ssm_out_weight_grad: float32 [1536, 1024], P('fsdp')
- attn_out_weight_grad: float32 [512, 1024], P('fsdp')
- decay_log_grad: float32 [24], replicated
- step_bias_grad: float32 [24], replicated
- skip_gain_grad: float32 [24], replicated
- norm_gain_two_grad: float32 [1024], P('fsdp')
- gate_weight_grad: float32 [1024, 2048], P('fsdp')
- up_weight_grad: float32 [1024, 2048], P('fsdp')
- down_weight_grad: float32 [2048, 1024], P('fsdp')
The draws below stay inside these ranges and needn't reach their ends.
Inputs may be any that keep to these rules, and one draw needn't show every extreme that they name: `segments`: each sequence holds three documents: the middle one starts within the first 256 tokens and ends within the last 256 tokens; document numbers never fall along a sequence.
All inputs are finite; a program needn't handle non-finite values.
Results may differ from the reference program's by a relative error of at most 0.0095.
The reference program's roundings to bfloat16 on the way count: a program that leaves them out, or rounds other values in their place, can miss the bound.
Values may be sent and summed in bfloat16 or wider, within the bound.
No kernel may reach another device: no remote copies, remote signals or barrier semaphores. Data moves between devices by JAX's collectives and lax.ppermute only.
A program may use at most 192 MiB of HBM per device.

```python
from functools import partial
import jax
import jax.numpy as jnp
from jax import lax

D = 1024
FF = 2048
SSM_HEADS = 24
HEAD = 64
STATE = 128
Q_HEADS = 8
KV_HEADS = 2
TOK_DEV = 256
SEQ = 4096
SEQS = 2


def draw_segments(key, part):
    key = jax.random.fold_in(key, 7)
    first_key, second_key = jax.random.split(key, 2)
    begin_at = jax.random.randint(first_key, (SEQS, 1), 8, TOK_DEV // 2)
    finish_at = SEQ - jax.random.randint(second_key, (SEQS, 1), 8, TOK_DEV // 2)
    positions = jnp.arange(SEQ, dtype=jnp.int32)[None, :]
    return (positions >= begin_at).astype(jnp.int32) + (positions >= finish_at).astype(jnp.int32)


def block_levels(stream_key, dims, shards, low, largest):
    factor_of = 1.0
    for position, blocks in shards:
        draws = jax.random.uniform(jax.random.fold_in(jax.random.fold_in(stream_key, 6), position), (blocks,), jnp.float32, low / len(shards), largest / len(shards))
        factor_of = factor_of * jnp.repeat(jnp.exp(draws), dims[position] // blocks).reshape((-1,) + (1,) * (len(dims) - 1 - position))
    return factor_of


def centred(key, dims, deviation, reach, cuts=(), held_as=jnp.bfloat16):
    loudness = block_levels(key, dims, cuts, -0.22, 0.18) if cuts else 1.0
    values = jax.random.normal(key, dims, jnp.float32) * deviation * loudness
    return jnp.minimum(jnp.maximum(values, -reach), reach).astype(held_as)


def setup_inputs(seed: int = 0) -> dict:
    arg_keys = jax.random.split(jax.random.key(seed), 17)
    return {
        "tokens": centred(arg_keys[0], (SEQS, SEQ, D), 1.0, 6.0, ((0, 2), (1, 16))),
        "segments": draw_segments(jax.random.fold_in(arg_keys[16], 71), 0),
        "cotangent": centred(arg_keys[2], (SEQS, SEQ, D), 1.0, 6.0, ((0, 2), (1, 16))),
        "norm_gain_one": jnp.clip(1.0 + 0.1 * jax.random.normal(arg_keys[3], (D,), jnp.float32), 0.5, 1.5).astype(jnp.bfloat16),
        "in_weight": centred(arg_keys[4], (D, 2 * SSM_HEADS * HEAD + 2 * STATE), D ** -0.5, 0.1875, ((0, 16),)),
        "step_weight": centred(arg_keys[5], (D, SSM_HEADS), D ** -0.5, 0.1875, ((0, 16),)),
        "qkv_weight": centred(arg_keys[6], (D, Q_HEADS * HEAD + 2 * KV_HEADS * HEAD), D ** -0.5, 0.1875, ((0, 16),)),
        "ssm_out_weight": centred(arg_keys[7], (SSM_HEADS * HEAD, D), (64 * SSM_HEADS * HEAD) ** -0.5, 0.01953125, ((0, 16),)),
        "attn_out_weight": centred(arg_keys[8], (Q_HEADS * HEAD, D), 1 ** -0.5, 6.0, ((0, 16),)),
        "decay_log": jnp.clip(jax.random.uniform(arg_keys[9], (SSM_HEADS,), jnp.float32, -9.0, -1.0), -9.0, -1.0),
        "step_bias": jnp.clip(jax.random.uniform(arg_keys[10], (SSM_HEADS,), jnp.float32, -4.0, -1.0), -4.0, -1.0),
        "skip_gain": jnp.clip(jax.random.uniform(arg_keys[11], (SSM_HEADS,), jnp.float32, 0.5, 1.5), 0.5, 1.5),
        "norm_gain_two": jnp.clip(1.0 + 0.1 * jax.random.normal(arg_keys[12], (D,), jnp.float32), 0.5, 1.5).astype(jnp.bfloat16),
        "gate_weight": centred(arg_keys[13], (D, FF), D ** -0.5, 0.1875, ((0, 16),)),
        "up_weight": centred(arg_keys[14], (D, FF), D ** -0.5, 0.1875, ((0, 16),)),
        "down_weight": centred(arg_keys[15], (FF, D), FF ** -0.5, 0.125, ((0, 16),)),
    }


@jax.custom_vjp
def low(v):
    return lax.optimization_barrier(v.astype(jnp.bfloat16)).astype(jnp.float32)

@jax.custom_vjp
def low_back(v):
    return v

def low_keep(v):
    return (low(v), None)

def low_pass(kept, grad):
    return (grad,)

def back_keep(v):
    return (v, None)

def back_low(kept, grad):
    return (low(grad),)
low.defvjp(low_keep, low_pass)
low_back.defvjp(back_keep, back_low)
EPSILON = 1e-05
HIGHEST = lax.Precision.HIGHEST
NEGATIVE = -1e+30
QUERY_BLOCK = 512

def product(left, right):
    return jnp.dot(left, right, precision=HIGHEST, preferred_element_type=jnp.float32)

def normalize(values, gain_vec):
    inverse = lax.rsqrt(lax.optimization_barrier(jnp.mean(values * values, axis=-1, keepdims=True)) + EPSILON)
    return values * inverse * gain_vec

def ssm_block(decay_rate, skip_gain, carry_in, pieces):
    carry_state, seg_before = carry_in
    inputs, b_rows, c_rows, step_size, gate_z, segment = pieces
    cumulate = jnp.cumsum(-decay_rate[None, :] * step_size, axis=0)
    positions = jnp.arange(segment.shape[0])
    allowed = (segment[:, None] == segment[None, :]) & (positions[:, None] >= positions[None, :])
    allowed_f = allowed.astype(jnp.float32)[:, :, None]
    within = jnp.exp(jnp.where(allowed[:, :, None], cumulate[:, None, :] - cumulate[None, :, :], 0.0)) * allowed_f
    cross_cb = product(c_rows, b_rows.T)
    mixing = cross_cb[:, :, None] * within * step_size[None, :, :]
    direct = jnp.einsum('tsh,shp->thp', mixing, inputs, precision=HIGHEST)
    carried_on = (segment == seg_before).astype(jnp.float32)
    entry_gain = jnp.exp(cumulate) * carried_on[:, None]
    carried = jnp.einsum('hpn,tn->thp', carry_state, c_rows, precision=HIGHEST) * entry_gain[:, :, None]
    output = (direct + carried + skip_gain[None, :, None] * inputs) * jax.nn.silu(gate_z)
    last_same = (segment == segment[-1]).astype(jnp.float32)[:, None]
    weight_tail = jnp.exp(cumulate[-1][None, :] - cumulate) * last_same * step_size
    fresh_state = jnp.einsum('sh,shp,sn->hpn', weight_tail, inputs, b_rows, precision=HIGHEST)
    keep_factor = jnp.exp(cumulate[-1]) * carried_on[-1]
    return ((keep_factor[:, None, None] * carry_state + fresh_state, segment[-1]), output)

def ssm_sequence(inputs, b_rows, c_rows, step_size, gate_z, segment, decay_rate, skip_gain):
    blocks = SEQ // TOK_DEV
    shaped = (inputs.reshape(blocks, TOK_DEV, SSM_HEADS, HEAD), b_rows.reshape(blocks, TOK_DEV, STATE), c_rows.reshape(blocks, TOK_DEV, STATE), step_size.reshape(blocks, TOK_DEV, SSM_HEADS), gate_z.reshape(blocks, TOK_DEV, SSM_HEADS, HEAD), segment.reshape(blocks, TOK_DEV))
    start_state = (jnp.zeros((SSM_HEADS, HEAD, STATE), jnp.float32), jnp.array(-1, dtype=jnp.int32))
    finished, outputs = lax.scan(jax.checkpoint(partial(ssm_block, decay_rate, skip_gain)), start_state, shaped)
    return outputs.reshape(SEQ, SSM_HEADS * HEAD)

def attention(queries, keys_all, values_all, segment):
    q_scale = HEAD ** (-0.5)
    group_size = Q_HEADS // KV_HEADS
    blocks = SEQ // QUERY_BLOCK
    positions = jnp.arange(SEQ, dtype=jnp.int32)
    key_heads = keys_all.reshape(SEQ, KV_HEADS, HEAD)
    value_heads = values_all.reshape(SEQ, KV_HEADS, HEAD)

    def one_block(pieces):
        block_q, block_place, block_seg = pieces
        raw_scores = jnp.einsum('tkgd,jkd->kgtj', block_q, key_heads, precision=HIGHEST) * q_scale
        scores = low_back(raw_scores)
        allowed = (positions[None, :] <= block_place[:, None]) & (segment[None, :] == block_seg[:, None])
        scores = jnp.where(allowed[None, None], scores, NEGATIVE)
        log_total = jax.nn.logsumexp(scores, axis=-1, keepdims=True)
        weights_low = low(jnp.exp(scores - log_total))
        mixed_out = jnp.einsum('kgtj,jkd->tkgd', weights_low, value_heads, precision=HIGHEST)
        return mixed_out.reshape(QUERY_BLOCK, Q_HEADS * HEAD)
    pieces = (queries.reshape(blocks, QUERY_BLOCK, KV_HEADS, group_size, HEAD), positions.reshape(blocks, QUERY_BLOCK), segment.reshape(blocks, QUERY_BLOCK))
    outputs = lax.map(jax.checkpoint(one_block), pieces)
    return outputs.reshape(SEQ, Q_HEADS * HEAD)

def layer(inputs, segment, gain_one, in_weight, step_weight, qkv_weight, ssm_out_weight, attn_out_weight, decay_log, step_bias, skip_gain, gain_two, gate_weight, up_weight, down_weight):
    inner_width = SSM_HEADS * HEAD
    q_width = Q_HEADS * HEAD
    k_width = KV_HEADS * HEAD
    h_one = low(normalize(inputs, gain_one))
    ssm_in = low_back(product(h_one, in_weight))
    step_raw = low_back(product(h_one, step_weight))
    qkv_rows = low(low_back(product(h_one, qkv_weight)))
    gate_z = ssm_in[:, :inner_width].reshape(SEQ, SSM_HEADS, HEAD)
    ssm_x = ssm_in[:, inner_width:2 * inner_width].reshape(SEQ, SSM_HEADS, HEAD)
    b_rows = ssm_in[:, 2 * inner_width:2 * inner_width + STATE]
    c_rows = ssm_in[:, 2 * inner_width + STATE:]
    step_size = jax.nn.softplus(step_raw + step_bias)
    gated = ssm_sequence(ssm_x, b_rows, c_rows, step_size, gate_z, segment, jnp.exp(decay_log), skip_gain)
    ssm_branch = low_back(product(low(gated), ssm_out_weight))
    attended = attention(qkv_rows[:, :q_width], qkv_rows[:, q_width:q_width + k_width], qkv_rows[:, q_width + k_width:], segment)
    attn_branch = low_back(product(low(low_back(attended)), attn_out_weight))
    resid = inputs + ssm_branch + attn_branch
    h_two = low(normalize(resid, gain_two))
    gate_pre = low_back(product(h_two, gate_weight))
    up_pre = low_back(product(h_two, up_weight))
    activated = low(jax.nn.silu(gate_pre) * up_pre)
    return resid + low_back(product(activated, down_weight))

def reference(tokens, segments, cotangent, norm_gain_one, in_weight, step_weight, qkv_weight, ssm_out_weight, attn_out_weight, decay_log, step_bias, skip_gain, norm_gain_two, gate_weight, up_weight, down_weight):
    params = tuple((weight.astype(jnp.float32) for weight in (norm_gain_one, in_weight, step_weight, qkv_weight, ssm_out_weight, attn_out_weight, decay_log, step_bias, skip_gain, norm_gain_two, gate_weight, up_weight, down_weight)))

    def one_sequence(totals, pieces):
        inputs, segment, upstream = pieces

        def forward(values, *weights):
            return layer(values, segment, *weights)
        result, backward = jax.vjp(forward, inputs.astype(jnp.float32), *params)
        grads = backward(upstream.astype(jnp.float32))
        totals = tuple((total_now + grad_now for total_now, grad_now in zip(totals, grads[1:])))
        return (totals, (result.astype(jnp.bfloat16), grads[0].astype(jnp.bfloat16)))
    zero_grads = tuple((jnp.zeros_like(weight) for weight in params))
    totals, (outputs, input_grads) = lax.scan(one_sequence, zero_grads, (tokens, segments, cotangent))
    return (outputs, input_grads, totals[0], totals[1], totals[2], totals[3], totals[4], totals[5], totals[6], totals[7], totals[8], totals[9], totals[10], totals[11], totals[12])
```

```python
from functools import partial

import jax
import jax.numpy as jnp
from jax import lax
from jax.experimental import pallas as pl
from jax.experimental.pallas import tpu as pltpu
from jax.sharding import PartitionSpec as P

SSM_HEADS = 24
HEAD = 64
STATE = 128
Q_HEADS = 8
KV_HEADS = 2
SPLIT = 2
HEADS_HERE = SSM_HEADS // SPLIT
GROUP = Q_HEADS // KV_HEADS
INNER = HEADS_HERE * HEAD
EXTRA = 128

EPSILON = 1e-05
HIGHEST = lax.Precision.HIGHEST
NEGATIVE = -1e30
AXIS = "fsdp"


def to_low(values):
    return values.astype(jnp.bfloat16)


def matmul(left, right):
    return jnp.dot(left, right, preferred_element_type=jnp.float32)


def matmul_tn(left, right):
    return lax.dot_general(
        left, right, (((0,), (0,)), ((), ())), preferred_element_type=jnp.float32
    )


def matmul_nt(left, right):
    return lax.dot_general(
        left, right, (((1,), (1,)), ((), ())), preferred_element_type=jnp.float32
    )


def norm_back(grad_normed, normed, inverse):
    return inverse * (grad_normed - normed * jnp.mean(grad_normed * normed, axis=-1, keepdims=True))


def ring_order(chips):
    if chips % 4:
        return list(range(chips))
    wide = 2 if chips == 8 else 4
    if chips % wide:
        return list(range(chips))
    tall = chips // wide
    walk = [row * wide for row in range(tall)]
    for step, row in enumerate(reversed(range(tall))):
        columns = list(range(1, wide))
        if step % 2:
            columns.reverse()
        walk += [row * wide + column for column in columns]
    return walk


class Ring:
    def __init__(self, devices):
        self.chips = devices // SPLIT
        self.walk = ring_order(self.chips)
        place = [0] * self.chips
        for position, chip in enumerate(self.walk):
            place[chip] = position
        index = lax.axis_index(AXIS)
        self.core = lax.rem(index, SPLIT)
        self.chip = index // SPLIT
        self.walk_table = jnp.asarray(self.walk, jnp.int32)
        self.position = jnp.asarray(place, jnp.int32)[self.chip]
        ahead = []
        for position in range(self.chips):
            here, there = self.walk[position], self.walk[(position + 1) % self.chips]
            ahead += [(here * SPLIT + core, there * SPLIT + core) for core in range(SPLIT)]
        self.ahead = ahead
        self.back = [(there, here) for here, there in ahead]
        self.pair = [(device, device ^ 1) for device in range(devices)]

    def swap(self, value):
        return lax.ppermute(value, AXIS, self.pair)

    def chip_at(self, offset):
        return self.walk_table[lax.rem(self.position + offset + 2 * self.chips, self.chips)]

    def gather(self, block):
        chips = self.chips
        half = block.shape[-1] // 2
        everything = jnp.zeros((chips,) + block.shape, block.dtype)
        zeros = (0,) * block.ndim

        def put(whole, part, offset, start=0):
            return lax.dynamic_update_slice(
                whole, part[None], (self.chip_at(offset),) + zeros[:-1] + (start,)
            )

        everything = put(everything, block, 0)
        onward, backward = block, block
        for step in range(1, chips // 2):
            onward = lax.ppermute(onward, AXIS, self.ahead)
            backward = lax.ppermute(backward, AXIS, self.back)
            everything = put(everything, onward, -step)
            everything = put(everything, backward, step)
        onward = lax.ppermute(onward[..., :half], AXIS, self.ahead)
        backward = lax.ppermute(backward[..., half:], AXIS, self.back)
        everything = put(everything, onward, -(chips // 2))
        return put(everything, backward, chips // 2, half)

    def scatter(self, chunk_of, wire):
        chips = self.chips
        far = chunk_of(self.chip_at(chips // 2))
        half = far.shape[-1] // 2
        onward = lax.ppermute(far[..., :half].astype(wire), AXIS, self.ahead)
        backward = lax.ppermute(far[..., half:].astype(wire), AXIS, self.back)
        for step in range(chips // 2 - 1, 0, -1):
            own = chunk_of(self.chip_at(step))
            if step == chips // 2 - 1:
                own = jnp.concatenate(
                    [own[..., :half] + onward.astype(jnp.float32), own[..., half:]], axis=-1
                )
            else:
                own = own + onward.astype(jnp.float32)
            onward = lax.ppermute(own.astype(wire), AXIS, self.ahead)
            own = chunk_of(self.chip_at(-step))
            if step == chips // 2 - 1:
                own = jnp.concatenate(
                    [own[..., :half], own[..., half:] + backward.astype(jnp.float32)], axis=-1
                )
            else:
                own = own + backward.astype(jnp.float32)
            backward = lax.ppermute(own.astype(wire), AXIS, self.back)
        return chunk_of(self.chip) + onward.astype(jnp.float32) + backward.astype(jnp.float32)


def exchange_sum(value, axis, size, first=1):
    hop = first
    while hop < size:
        partner = [(device, device ^ hop) for device in range(size)]
        value = value + lax.ppermute(value, axis, partner)
        hop *= 2
    return value


def replica_sum(value, size, wire):
    hop = 1
    while hop < size:
        partner = [(device, device ^ hop) for device in range(size)]
        sent = value.astype(wire)
        value = sent.astype(jnp.float32) + lax.ppermute(sent, "replica", partner).astype(
            jnp.float32
        )
        hop *= 2
    return value


def masked_scores(keys, queries, key_seg, query_seg, diagonal):
    scores = matmul_nt(keys, queries) * (HEAD**-0.5)
    allowed = key_seg == query_seg
    if diagonal:
        key_at = lax.broadcasted_iota(jnp.int32, scores.shape, 0)
        query_at = lax.broadcasted_iota(jnp.int32, scores.shape, 1)
        allowed = allowed & (key_at <= query_at)
    return jnp.where(allowed, scores, NEGATIVE)


def attention_forward_kernel(
    chip_ref, q_ref, kv_ref, key_seg_ref, query_seg_ref, out_ref, lse_ref, top, total, mixed
):
    chip = chip_ref[0]
    rows = q_ref.shape[1]
    query_seg = query_seg_ref[...]
    top[...] = jnp.full(top.shape, NEGATIVE, jnp.float32)
    total[...] = jnp.zeros(total.shape, jnp.float32)
    mixed[...] = jnp.zeros(mixed.shape, jnp.float32)

    def block(at, diagonal):
        begin = pl.multiple_of(at * rows, rows)
        keys = kv_ref[0, pl.ds(begin, rows), :]
        values = kv_ref[1, pl.ds(begin, rows), :]
        key_seg = key_seg_ref[pl.ds(begin, rows), :]
        for head in range(GROUP):
            scores = masked_scores(keys, q_ref[head], key_seg, query_seg, diagonal)
            before = top[head : head + 1, :]
            now = jnp.maximum(before, jnp.max(scores, axis=0, keepdims=True))
            weights = jnp.where(scores > 0.5 * NEGATIVE, jnp.exp(scores - now), 0.0)
            shrink = jnp.exp(before - now)
            top[head : head + 1, :] = now
            total[head : head + 1, :] = total[head : head + 1, :] * shrink + jnp.sum(
                weights, axis=0, keepdims=True
            )
            mixed[head] = mixed[head] * shrink + matmul_tn(values, to_low(weights))

    lax.fori_loop(0, chip, lambda at, unused: (block(at, False), unused)[1], 0)
    block(chip, True)
    for head in range(GROUP):
        share = total[head : head + 1, :]
        lse_ref[head : head + 1, :] = top[head : head + 1, :] + jnp.log(share)
        out_ref[head] = to_low(mixed[head] / share)


def attention_backward_kernel(
    chip_ref,
    q_ref,
    do_ref,
    kv_ref,
    key_seg_ref,
    query_seg_ref,
    lse_ref,
    delta_ref,
    dq_ref,
    dkv_ref,
    dq_sum,
):
    chip = chip_ref[0]
    rows = q_ref.shape[1]
    query_seg = query_seg_ref[...]
    scale = HEAD**-0.5
    dq_sum[...] = jnp.zeros(dq_sum.shape, jnp.float32)

    def block(at, diagonal):
        begin = pl.multiple_of(at * rows, rows)
        keys = kv_ref[0, pl.ds(begin, rows), :]
        values = kv_ref[1, pl.ds(begin, rows), :]
        key_seg = key_seg_ref[pl.ds(begin, rows), :]
        dk = jnp.zeros((rows, HEAD), jnp.float32)
        dv = jnp.zeros((rows, HEAD), jnp.float32)
        for head in range(GROUP):
            queries, outs = q_ref[head], do_ref[head]
            scores = masked_scores(keys, queries, key_seg, query_seg, diagonal)
            weights = jnp.exp(scores - lse_ref[head : head + 1, :])
            d_weights = matmul_nt(values, outs)
            d_scores = to_low(weights * (d_weights - delta_ref[head : head + 1, :]))
            dk = dk + matmul(d_scores, queries)
            dv = dv + matmul(to_low(weights), outs)
            dq_sum[head] = dq_sum[head] + matmul_tn(keys, d_scores)
        dkv_ref[0, pl.ds(begin, rows), :] = dk * scale
        dkv_ref[1, pl.ds(begin, rows), :] = dv

    lax.fori_loop(0, chip, lambda at, unused: (block(at, False), unused)[1], 0)
    block(chip, True)

    def clear(at, unused):
        begin = pl.multiple_of(at * rows, rows)
        dkv_ref[:, pl.ds(begin, rows), :] = jnp.zeros((2, rows, HEAD), jnp.float32)
        return unused

    lax.fori_loop(chip + 1, kv_ref.shape[1] // rows, clear, 0)
    for head in range(GROUP):
        dq_ref[head] = to_low(dq_sum[head] * scale)


def in_smem():
    return pl.BlockSpec(memory_space=pltpu.SMEM)


def in_vmem():
    return pl.BlockSpec(memory_space=pltpu.VMEM)


def attention_forward(chip, queries, kv, key_seg, query_seg):
    rows = queries.shape[1]
    return pl.pallas_call(
        attention_forward_kernel,
        out_shape=(
            jax.ShapeDtypeStruct((GROUP, HEAD, rows), jnp.bfloat16),
            jax.ShapeDtypeStruct((GROUP, rows), jnp.float32),
        ),
        in_specs=[in_smem()] + [in_vmem()] * 4,
        out_specs=(in_vmem(), in_vmem()),
        scratch_shapes=[
            pltpu.VMEM((GROUP, rows), jnp.float32),
            pltpu.VMEM((GROUP, rows), jnp.float32),
            pltpu.VMEM((GROUP, HEAD, rows), jnp.float32),
        ],
        compiler_params=pltpu.CompilerParams(vmem_limit_bytes=40 * 2**20),
        name="attention_forward",
    )(chip, queries, kv, key_seg, query_seg)


def attention_backward(chip, queries, d_out, kv, key_seg, query_seg, lse, delta):
    rows = queries.shape[1]
    return pl.pallas_call(
        attention_backward_kernel,
        out_shape=(
            jax.ShapeDtypeStruct((GROUP, HEAD, rows), jnp.bfloat16),
            jax.ShapeDtypeStruct(kv.shape, jnp.float32),
        ),
        in_specs=[in_smem()] + [in_vmem()] * 7,
        out_specs=(in_vmem(), in_vmem()),
        scratch_shapes=[pltpu.VMEM((GROUP, HEAD, rows), jnp.float32)],
        compiler_params=pltpu.CompilerParams(vmem_limit_bytes=40 * 2**20),
        name="attention_backward",
    )(chip, queries, d_out, kv, key_seg, query_seg, lse, delta)


def decays(step_raw, decay_log, step_bias):
    step_size = jax.nn.softplus(step_raw + step_bias)
    cumulate = jnp.cumsum(-jnp.exp(decay_log) * step_size, axis=1)
    return (step_size, cumulate)


def ssm_summary(inputs, b_rows, step_raw, decay_log, step_bias, segment, previous):
    step_size, cumulate = decays(step_raw, decay_log, step_bias)
    carried_on = (segment == previous[:, None]).astype(jnp.float32)
    last_same = (segment == segment[:, -1:]).astype(jnp.float32)[:, :, None]
    weight_tail = jnp.exp(cumulate[:, -1:] - cumulate) * last_same * step_size
    weighted = inputs * weight_tail[..., None]
    fresh = jnp.einsum("kshp,ksn->khpn", weighted, b_rows, precision=HIGHEST)
    keep = jnp.exp(cumulate[:, -1]) * carried_on[:, -1:]
    chip_fresh, chip_keep = fresh[0], keep[0]
    for at in range(1, fresh.shape[0]):
        chip_fresh = keep[at][:, None, None] * chip_fresh + fresh[at]
        chip_keep = keep[at] * chip_keep
    return (chip_fresh, chip_keep, fresh, keep)


def ssm_output(
    state_in,
    fresh,
    keep,
    inputs,
    b_rows,
    c_rows,
    step_raw,
    decay_log,
    step_bias,
    skip_gain,
    gate_z,
    segment,
    previous,
):
    states = [state_in]
    for at in range(1, fresh.shape[0]):
        states.append(keep[at - 1][:, None, None] * states[-1] + fresh[at - 1])
    states = jnp.stack(states)
    step_size, cumulate = decays(step_raw, decay_log, step_bias)
    positions = jnp.arange(segment.shape[1])
    allowed = (segment[:, :, None] == segment[:, None, :]) & (
        positions[:, None] >= positions[None, :]
    )
    allowed_f = allowed.astype(jnp.float32)[:, None]
    by_head = cumulate.transpose(0, 2, 1)
    within = (
        jnp.exp(jnp.where(allowed[:, None], by_head[:, :, :, None] - by_head[:, :, None, :], 0.0))
        * allowed_f
    )
    cross_cb = jnp.einsum("ktn,ksn->kts", c_rows, b_rows, precision=HIGHEST)
    mixing = cross_cb[:, None] * within * step_size.transpose(0, 2, 1)[:, :, None, :]
    direct = jnp.einsum("khts,kshp->kthp", mixing, inputs, precision=HIGHEST)
    carried_on = (segment == previous[:, None]).astype(jnp.float32)
    entry_gain = jnp.exp(cumulate) * carried_on[:, :, None]
    carried = (
        jnp.einsum("khpn,ktn->kthp", states, c_rows, precision=HIGHEST) * entry_gain[..., None]
    )
    return (direct + carried + skip_gain[:, None] * inputs) * jax.nn.silu(gate_z)


def on_device(
    devices,
    replicas,
    tokens,
    segments,
    cotangent,
    norm_gain_one,
    in_weight,
    step_weight,
    qkv_weight,
    ssm_out_weight,
    attn_out_weight,
    decay_log,
    step_bias,
    skip_gain,
    norm_gain_two,
    gate_weight,
    up_weight,
    down_weight,
):
    ring = Ring(devices)
    chips, core, chip = ring.chips, ring.core, ring.chip
    first = core == 0
    tok_rows = tokens.shape[1]
    rows = SPLIT * tok_rows
    shard, width = in_weight.shape[0], tokens.shape[2]
    hidden = gate_weight.shape[1]
    slab = hidden // devices
    ff_here = hidden // SPLIT
    ssm_rows, attn_rows = ssm_out_weight.shape[0], attn_out_weight.shape[0]
    half_width = width // SPLIT
    ssm_width = SSM_HEADS * HEAD
    q_width, k_width = Q_HEADS * HEAD, KV_HEADS * HEAD
    q_here = GROUP * HEAD

    def mine(value, axis, which):
        size = value.shape[axis] // SPLIT
        return lax.dynamic_slice_in_dim(value, which * size, size, axis)

    def in_order(own, other, axis):
        return jnp.where(
            first,
            jnp.concatenate([own, other], axis=axis),
            jnp.concatenate([other, own], axis=axis),
        )

    def mixer_columns(which):
        ends = in_weight[:, 2 * ssm_width :]
        near = mine(ends, 1, which)
        far = mine(ends, 1, 1 - which)
        gains = jnp.stack([norm_gain_one, norm_gain_two], axis=1)
        extra = jnp.concatenate(
            [
                mine(step_weight, 1, which),
                gains,
                jnp.zeros((shard, EXTRA - HEADS_HERE - 2), jnp.bfloat16),
            ],
            axis=1,
        )
        return jnp.concatenate(
            [
                mine(in_weight[:, :ssm_width], 1, which),
                mine(in_weight[:, ssm_width : 2 * ssm_width], 1, which),
                near,
                far,
                mine(qkv_weight[:, :q_width], 1, which),
                mine(qkv_weight[:, q_width : q_width + k_width], 1, which),
                mine(qkv_weight[:, q_width + k_width :], 1, which),
                extra,
            ],
            axis=1,
        )

    mixer_own = in_order(mixer_columns(core), ring.swap(mixer_columns(1 - core)), 0)
    token_pair = in_order(tokens[0], ring.swap(tokens[0]), 0)
    upstream = in_order(cotangent[0], ring.swap(cotangent[0]), 0)
    w_mix = ring.gather(mixer_own).reshape(width, -1)

    out_shard = jnp.concatenate([ssm_out_weight, attn_out_weight], axis=0)
    out_shard = in_order(mine(out_shard, 1, core), ring.swap(mine(out_shard, 1, 1 - core)), 0)

    def ff_columns(which):
        parts = [
            lax.dynamic_index_in_dim(
                weight.reshape(shard, chips, SPLIT, slab), which, axis=2, keepdims=False
            ).reshape(shard, ff_here)
            for weight in (gate_weight, up_weight)
        ]
        return jnp.concatenate(parts, axis=1)

    ff_own = in_order(ff_columns(core), ring.swap(ff_columns(1 - core)), 0)

    seg_all = segments[0]
    first_row = chip * rows
    seg_mine = lax.dynamic_slice_in_dim(seg_all, first_row, rows)
    seg_blocks = seg_mine.reshape(SPLIT, tok_rows)
    before = jnp.where(
        first_row > 0,
        lax.dynamic_index_in_dim(seg_all, jnp.maximum(first_row - 1, 0), keepdims=False),
        -1,
    )
    seg_before = jnp.concatenate([before[None], seg_blocks[:-1, -1]])
    chip_scalar = chip.astype(jnp.int32).reshape(1)

    inputs = token_pair.astype(jnp.float32)
    extras = w_mix[:, -EXTRA:]
    gain_one = extras[:, HEADS_HERE].astype(jnp.float32)
    gain_two = extras[:, HEADS_HERE + 1].astype(jnp.float32)
    inverse_one = lax.rsqrt(jnp.mean(inputs * inputs, axis=-1, keepdims=True) + EPSILON)
    normed_one = inputs * inverse_one
    h_one = to_low(normed_one * gain_one)
    projected = matmul(h_one, w_mix)
    z_end, u_end = INNER, 2 * INNER
    near_end, far_end = u_end + STATE, u_end + 2 * STATE
    q_end = far_end + q_here
    k_end, v_end = q_end + HEAD, q_end + 2 * HEAD
    gate_z = projected[:, :z_end].reshape(SPLIT, tok_rows, HEADS_HERE, HEAD)
    ssm_x = projected[:, z_end:u_end].reshape(SPLIT, tok_rows, HEADS_HERE, HEAD)
    near, far = projected[:, u_end:near_end], projected[:, near_end:far_end]
    b_rows = jnp.where(first, near, far).reshape(SPLIT, tok_rows, STATE)
    c_rows = jnp.where(first, far, near).reshape(SPLIT, tok_rows, STATE)
    step_raw = projected[:, v_end : v_end + HEADS_HERE].reshape(SPLIT, tok_rows, HEADS_HERE)
    decay_here, bias_here, skip_here = (
        mine(decay_log, 0, core),
        mine(step_bias, 0, core),
        mine(skip_gain, 0, core),
    )

    kv_own = to_low(projected[:, q_end:v_end]).reshape(rows, 2, HEAD).transpose(1, 0, 2)
    kv_all = ring.gather(kv_own.reshape(2 * rows // 2, 2 * HEAD))
    kv_all = (
        kv_all.reshape(chips, 2, rows, HEAD).transpose(1, 0, 2, 3).reshape(2, chips * rows, HEAD)
    )

    summary_fn = partial(ssm_summary, segment=seg_blocks, previous=seg_before)
    (chip_fresh, chip_keep, fresh, keep), summary_back = jax.vjp(
        summary_fn, ssm_x, b_rows, step_raw, decay_here, bias_here
    )

    def pack_state(state, factor):
        tail = jnp.zeros((8, STATE), jnp.float32).at[0, :HEADS_HERE].set(factor)
        return jnp.concatenate([state.reshape(HEADS_HERE * HEAD, STATE), tail], axis=0)

    places = jnp.arange(chips, dtype=jnp.int32)

    def chained(packed, keeps, reverse):
        state = packed[:, : HEADS_HERE * HEAD].reshape(chips, HEADS_HERE, HEAD, STATE)
        total = jnp.zeros((HEADS_HERE,), jnp.float32)
        weights = [None] * chips
        running = jnp.ones((HEADS_HERE,), jnp.float32)
        for at in range(chips) if reverse else reversed(range(chips)):
            beyond = at > chip if reverse else at < chip
            weights[at] = jnp.where(beyond, running, 0.0)
            running = jnp.where(beyond, running * keeps[at], running)
        return jnp.einsum("kh,khpn->hpn", jnp.stack(weights), state, precision=HIGHEST)

    packed = ring.gather(pack_state(chip_fresh, chip_keep))
    keeps = packed[:, HEADS_HERE * HEAD, :HEADS_HERE]
    state_in = chained(packed, keeps, False)

    queries = to_low(projected[:, far_end:q_end]).reshape(rows, GROUP, HEAD).transpose(1, 0, 2)
    key_seg = seg_all[:, None]
    query_seg = seg_mine[None, :]
    attended_t, lse = attention_forward(chip_scalar, queries, kv_all, key_seg, query_seg)
    attended_low = attended_t.transpose(2, 0, 1).reshape(rows, q_here)

    output_fn = partial(ssm_output, segment=seg_blocks, previous=seg_before)
    gated, output_back = jax.vjp(
        output_fn,
        state_in,
        fresh,
        keep,
        ssm_x,
        b_rows,
        c_rows,
        step_raw,
        decay_here,
        bias_here,
        skip_here,
        gate_z,
    )
    gated_low = to_low(gated.reshape(rows, INNER))

    out_half = ring.gather(out_shard).reshape(chips * SPLIT, ssm_rows + attn_rows, half_width)
    out_ssm = out_half[:, :ssm_rows].reshape(devices * ssm_rows, half_width)
    out_attn = out_half[:, ssm_rows:].reshape(devices * attn_rows, half_width)

    def out_rows(which):
        return jnp.concatenate([mine(out_ssm, 0, which), mine(out_attn, 0, which)], axis=0)

    w_out = in_order(out_rows(core), ring.swap(out_rows(1 - core)), 1)
    mixed = jnp.concatenate([gated_low, attended_low], axis=1)
    branch = matmul(mixed, w_out)
    resid = inputs + (branch + ring.swap(branch))

    w_ff = ring.gather(ff_own).reshape(width, SPLIT * ff_here)
    w_down = ring.gather(down_weight).reshape(ff_here, width)
    inverse_two = lax.rsqrt(jnp.mean(resid * resid, axis=-1, keepdims=True) + EPSILON)
    normed_two = resid * inverse_two
    h_two = to_low(normed_two * gain_two)
    gate_up = matmul(h_two, w_ff)
    gate_pre, up_pre = gate_up[:, :ff_here], gate_up[:, ff_here:]
    sigmoid_gate = jax.nn.sigmoid(gate_pre)
    activated = to_low(gate_pre * sigmoid_gate * up_pre)
    partial_out = matmul(activated, w_down)
    result = (
        mine(resid, 0, core) + mine(partial_out, 0, core) + ring.swap(mine(partial_out, 0, 1 - core))
    )
    d_act = matmul_nt(upstream, w_down)
    d_gate = to_low(d_act * up_pre * sigmoid_gate * (1.0 + gate_pre * (1.0 - sigmoid_gate)))
    d_up = to_low(d_act * gate_pre * sigmoid_gate)
    d_gate_up = jnp.concatenate([d_gate, d_up], axis=1)
    d_h_two = matmul_nt(d_gate_up, w_ff)
    d_h_two = d_h_two + ring.swap(d_h_two)
    g_norm_two = 0.5 * jnp.sum(d_h_two * normed_two, axis=0)
    d_resid = upstream.astype(jnp.float32) + norm_back(d_h_two * gain_two, normed_two, inverse_two)
    d_branch = to_low(d_resid)

    def chunks(grad):
        pieces = grad.reshape((chips, -1) + grad.shape[1:])
        return lambda at: lax.dynamic_index_in_dim(pieces, at, keepdims=False)

    g_down = matmul_tn(activated, upstream)
    g_ff = matmul_tn(h_two, d_gate_up)
    down_sum = ring.scatter(chunks(g_down), jnp.bfloat16)
    ff_sum = ring.scatter(chunks(g_ff), jnp.bfloat16)

    d_mixed = matmul_nt(d_branch, w_out)
    d_gated = d_mixed[:, :INNER]
    d_att = to_low(d_mixed[:, INNER:])
    d_heads = d_att.reshape(rows, GROUP, HEAD).transpose(1, 0, 2)
    delta = jnp.sum(
        attended_low.astype(jnp.float32).reshape(rows, GROUP, HEAD)
        * d_att.astype(jnp.float32).reshape(rows, GROUP, HEAD),
        axis=-1,
    ).T
    dq_t, dkv = attention_backward(
        chip_scalar, queries, d_heads, kv_all, key_seg, query_seg, lse, delta
    )
    dkv_pieces = dkv.reshape(2, chips, rows, HEAD)

    def dkv_chunk(at):
        return lax.dynamic_index_in_dim(dkv_pieces, at, axis=1, keepdims=False).reshape(
            rows, 2 * HEAD
        )

    dkv_sum = ring.scatter(dkv_chunk, jnp.float32)
    dkv_low = to_low(dkv_sum.reshape(2, rows, HEAD).transpose(1, 0, 2).reshape(rows, 2 * HEAD))
    dq_low = dq_t.transpose(2, 0, 1).reshape(rows, q_here)

    grads_y = output_back(d_gated.reshape(SPLIT, tok_rows, HEADS_HERE, HEAD))
    later = ring.gather(pack_state(grads_y[0], chip_keep))
    later_grad = chained(later, keeps, True)
    grads_s = summary_back(
        (later_grad, jnp.sum(later_grad * state_in, axis=(1, 2)), grads_y[1], grads_y[2])
    )
    d_z = to_low(grads_y[10].reshape(rows, INNER))
    d_u = to_low((grads_y[3] + grads_s[0]).reshape(rows, INNER))
    d_b = (grads_y[4] + grads_s[1]).reshape(rows, STATE)
    d_c = grads_y[5].reshape(rows, STATE)
    d_near = to_low(jnp.where(first, d_b, d_c) + ring.swap(jnp.where(first, d_c, d_b)))
    d_step = to_low((grads_y[6] + grads_s[2]).reshape(rows, HEADS_HERE))
    head_grads = jnp.stack([grads_y[7] + grads_s[3], grads_y[8] + grads_s[4], grads_y[9]])
    d_step_wide = jnp.pad(d_step, ((0, 0), (0, EXTRA - HEADS_HERE)))
    d_projected = jnp.concatenate([d_z, d_u, d_near, dq_low, dkv_low, d_step_wide], axis=1)
    w_back = jnp.concatenate([w_mix[:, :near_end], w_mix[:, far_end:]], axis=1)

    g_out = matmul_tn(mixed, d_branch)
    g_mix = matmul_tn(h_one, d_projected)
    mix_sum = ring.scatter(chunks(g_mix), jnp.bfloat16)
    g_half = in_order(mine(g_out, 1, core), ring.swap(mine(g_out, 1, 1 - core)), 0)
    g_ssm = jnp.concatenate([g_half[:INNER], g_half[INNER + q_here : 2 * INNER + q_here]], axis=0)
    g_attn = jnp.concatenate([g_half[INNER : INNER + q_here], g_half[2 * INNER + q_here :]], axis=0)
    g_joint = jnp.concatenate(
        [
            g_ssm.reshape(devices, ssm_rows, half_width),
            g_attn.reshape(devices, attn_rows, half_width),
        ],
        axis=1,
    )
    out_sum = ring.scatter(
        chunks(g_joint.reshape(devices * (ssm_rows + attn_rows), half_width)), jnp.bfloat16
    )

    d_h_one = matmul_nt(d_projected, w_back)
    d_h_one = mine(d_h_one, 0, core) + ring.swap(mine(d_h_one, 0, 1 - core))
    normed_own = mine(normed_one, 0, core)
    g_norm_one = jnp.sum(d_h_one * normed_own, axis=0)
    d_inputs = mine(d_resid, 0, core) + norm_back(
        d_h_one * gain_one, normed_own, mine(inverse_one, 0, core)
    )

    def owned(total, axis=0):
        keep_part = mine(total, axis, core)
        other_part = ring.swap(mine(total, axis, 1 - core))
        return (
            jnp.where(first, keep_part, other_part),
            jnp.where(first, other_part, keep_part),
        )

    def whole(total):
        return replica_sum(total, replicas, jnp.bfloat16)

    down_grad = whole(down_sum)
    low_ff, high_ff = owned(whole(ff_sum))

    def interleave(low, high):
        return jnp.stack(
            [low.reshape(shard, chips, slab), high.reshape(shard, chips, slab)], axis=2
        ).reshape(shard, hidden)

    gate_grad = interleave(low_ff[:, :ff_here], high_ff[:, :ff_here])
    up_grad = interleave(low_ff[:, ff_here:], high_ff[:, ff_here:])
    low_out, high_out = owned(whole(out_sum))
    out_grad = jnp.concatenate([low_out, high_out], axis=1)
    low_mix, high_mix = owned(whole(mix_sum))

    def both(begin, end):
        return [low_mix[:, begin:end], high_mix[:, begin:end]]

    in_grad = jnp.concatenate(both(0, z_end) + both(z_end, u_end) + both(u_end, near_end), axis=1)
    q_at = near_end + q_here
    qkv_grad = jnp.concatenate(
        both(near_end, q_at) + both(q_at, q_at + HEAD) + both(q_at + HEAD, q_at + 2 * HEAD), axis=1
    )
    step_at = q_at + 2 * HEAD
    step_grad = jnp.concatenate(both(step_at, step_at + HEADS_HERE), axis=1)

    zeros = jnp.zeros_like(head_grads)
    head_wide = jnp.where(
        first,
        jnp.concatenate([head_grads, zeros], axis=1),
        jnp.concatenate([zeros, head_grads], axis=1),
    )
    small = jnp.concatenate([g_norm_one, g_norm_two, head_wide.reshape(-1)])
    small = exchange_sum(small, AXIS, devices)
    small = exchange_sum(small, "replica", replicas)
    index = lax.axis_index(AXIS)
    norm_one_grad = lax.dynamic_slice_in_dim(small, index * shard, shard)
    norm_two_grad = lax.dynamic_slice_in_dim(small, width + index * shard, shard)
    heads = small[2 * width :].reshape(3, SSM_HEADS)

    return (
        to_low(result)[None],
        to_low(d_inputs)[None],
        norm_one_grad,
        in_grad,
        step_grad,
        qkv_grad,
        out_grad[:ssm_rows],
        out_grad[ssm_rows:],
        heads[0],
        heads[1],
        heads[2],
        norm_two_grad,
        gate_grad,
        up_grad,
        down_grad,
    )


def solution(mesh):
    rows = P("fsdp", None)
    per_token = P("replica", "fsdp", None)
    vector = P("fsdp")
    return jax.shard_map(
        partial(on_device, mesh.shape["fsdp"], mesh.shape["replica"]),
        mesh=mesh,
        in_specs=(
            per_token,
            P("replica", None),
            per_token,
            vector,
            rows,
            rows,
            rows,
            rows,
            rows,
            P(),
            P(),
            P(),
            vector,
            rows,
            rows,
            rows,
        ),
        out_specs=(
            per_token,
            per_token,
            vector,
            rows,
            rows,
            rows,
            rows,
            rows,
            P(),
            P(),
            P(),
            vector,
            rows,
            rows,
            rows,
        ),
        check_vma=False,
    )
```
